512 devices in a mesh: row: 16 (over z, core), col: 32 (over y, x).
Axes of the slice: x: 4, y: 8, z: 8, core: 2. Of those that a mesh axis runs over, the one named last changes fastest.
Arguments:
- primal: float32 [8, 131072], P(None, ('col', 'row')), may hold values from 0 to 0.5
- dual: float32 [8, 131072], P(None, ('row', 'col')), may hold values from 0 to 1
- cost: float32 [8, 131072], P(None, ('col', 'row')), may hold values from -6 to 6
- upper: float32 [131072], P(('col', 'row')), may hold values from 0.25 to 1.5
- rhs: float32 [131072], P(('row', 'col')), may hold values from -6 to 6
- row_kind: int32 [131072], P(('row', 'col')), may hold values 0 or 1
- tiles: bfloat16 [24576, 128, 128], P(('row', 'col')), may hold values from -0.125 to 0.125
- tile_rows: int32 [24576], P(('row', 'col')), may hold values from 0 to 63, as said below
- tile_cols: int32 [24576], P(('row', 'col')), may hold values from 0 to 31
- tile_count: int32 [512], P(('row', 'col')), may hold values from 1 to 48, as said below
Outputs:
- primal_out: float32 [8, 131072], P(None, ('col', 'row'))
- dual_out: float32 [8, 131072], P(None, ('row', 'col'))
The draws below stay inside these ranges and needn't reach their ends.
Inputs may be any that keep to these rules, and one draw needn't show every extreme that they name: Within one device's slots the pairs (tile_rows, tile_cols) are all different. `tile_count`: some device has all 48 slots live in every draw; which one varies.
All inputs are finite; a program needn't handle non-finite values. No bound on the sum of `row_kind` on one device may be relied on, other than what follows from the above.
Results may differ from the reference program's by a relative error of at most 0.0012.
Values may be sent and summed in bfloat16 or wider, within the bound.
No kernel may reach another device: no remote copies, remote signals or barrier semaphores. Data moves between devices by JAX's collectives and lax.ppermute only.
A program may use at most 64 MiB of HBM per device.

```python
import jax
import jax.numpy as jnp
from jax import lax

REALIZATIONS = 8
ROWT = 64
COLT = 32
TILES_DEV = 48
ITERS = 2
NVAR = 131072
NCON = 131072
N_ROW = 16
N_COL = 32


def tile_positions(key):
    keys = jax.random.split(key, N_ROW * N_COL)

    def one_device(single):
        return jax.random.permutation(single, ROWT * COLT)[:TILES_DEV]
    return jax.vmap(one_device)(keys).reshape(-1).astype(jnp.int32)


def draw_tile_rows(key, part):
    return (tile_positions(key) // COLT).astype(jnp.int32)


def draw_tile_cols(key, part):
    return (tile_positions(key) % COLT).astype(jnp.int32)


def draw_tile_count(key, part):
    key = jax.random.fold_in(key, 5)
    first_key, second_key = jax.random.split(key)
    lowest = max(1, TILES_DEV // 4)
    counts = jax.random.randint(first_key, (N_ROW * N_COL,), lowest, TILES_DEV + 1)
    busiest = jax.random.randint(second_key, (), 0, N_ROW * N_COL)
    return counts.at[busiest].set(TILES_DEV).astype(jnp.int32)


def set_ends(result, own_key, smallest, largest):
    spot = [jax.random.randint(jax.random.fold_in(own_key, axis), (), 0, length) for axis, length in enumerate(result.shape)]
    widest = result.shape.index(max(result.shape))
    beside = spot[:widest] + [(spot[widest] + 1) % result.shape[widest]] + spot[widest + 1:]
    return result.at[tuple(spot)].set(smallest).at[tuple(beside)].set(largest)


def steps_of(key, shape, cuts, least, largest):
    loudness = 1.0
    for dim, parts in cuts:
        steps = jax.random.uniform(jax.random.fold_in(jax.random.fold_in(key, 6), dim), (parts,), jnp.float32, least / len(cuts), largest / len(cuts))
        loudness = loudness * jnp.repeat(jnp.exp(steps), shape[dim] // parts).reshape((-1,) + (1,) * (len(shape) - 1 - dim))
    return loudness


def normal_values(rng, extent, scale, bound, cuts=(), held_as=jnp.bfloat16):
    result = jax.random.normal(rng, extent, jnp.float32) * scale
    if len(cuts) > 0:
        result = steps_of(rng, extent, cuts, -0.22, 0.18) * result
    return jnp.clip(result, min=-bound, max=bound).astype(held_as)


def setup_inputs(seed: int = 0) -> dict:
    key_list = jax.random.split(jax.random.key(seed), 11)
    return {
        "primal": jnp.clip(0.5 * jax.random.uniform(key_list[0], (REALIZATIONS, NVAR), jnp.float32) ** steps_of(key_list[0], (REALIZATIONS, NVAR), ((1, 512),), -0.2, 0.2), 0.0, 0.5),
        "dual": jnp.clip(1.0 * jax.random.uniform(key_list[1], (REALIZATIONS, NCON), jnp.float32) ** steps_of(key_list[1], (REALIZATIONS, NCON), ((1, 512),), -0.2, 0.2), 0.0, 1.0),
        "cost": normal_values(key_list[2], (REALIZATIONS, NVAR), 1.0, 6.0, ((1, 512),), jnp.float32),
        "upper": jnp.clip(0.25 + 1.25 * jax.random.uniform(key_list[3], (NVAR,), jnp.float32) ** steps_of(key_list[3], (NVAR,), ((0, 512),), -0.2, 0.2), 0.25, 1.5),
        "rhs": normal_values(key_list[4], (NCON,), 1.0, 6.0, ((0, 512),), jnp.float32),
        "row_kind": set_ends((jax.random.randint(key_list[5], (NCON,), 0, 4) < 3).astype(jnp.int32), jax.random.fold_in(key_list[5], 1), 0, 1),
        "tiles": normal_values(key_list[6], (N_ROW * N_COL * TILES_DEV, 128, 128), (N_COL * TILES_DEV * 80 // ROWT) ** -0.5, 0.125, ((0, 512),)),
        "tile_rows": draw_tile_rows(jax.random.fold_in(key_list[10], 71), 0),
        "tile_cols": draw_tile_cols(jax.random.fold_in(key_list[10], 71), 0),
        "tile_count": draw_tile_count(jax.random.fold_in(key_list[10], 71), 0),
    }


PRIMAL_STEP = 0.4
DUAL_STEP = 0.4


def reference(primal, dual, cost, upper, rhs, row_kind, tiles, tile_rows, tile_cols, tile_count):
    width = primal.shape[0]
    row_span = ROWT * 128
    col_span = COLT * 128
    devcount = N_ROW * N_COL
    tile_sets = tiles.reshape(devcount, TILES_DEV, 128, 128)
    row_sets = tile_rows.reshape(devcount, TILES_DEV)
    col_sets = tile_cols.reshape(devcount, TILES_DEV)
    slot_ids = jnp.arange(TILES_DEV, dtype=jnp.int32)
    live_sets = (slot_ids[None, :] < tile_count[:, None]).astype(jnp.float32)
    device_ids = jnp.arange(devcount, dtype=jnp.int32)
    row_ids = jnp.arange(ROWT, dtype=jnp.int32)
    col_ids = jnp.arange(COLT, dtype=jnp.int32)

    def forward(vector):
        def visit(total, item):
            device, block, rows_here, cols_here, live_here = item
            i_row = (device // N_COL).astype(jnp.int32)
            j_col = (device % N_COL).astype(jnp.int32)
            source = lax.dynamic_slice_in_dim(vector, j_col * col_span, col_span, 1)
            pieces = source.reshape(width, COLT, 128)[:, cols_here].astype(jnp.float32)
            contrib = jnp.einsum('rtk,tjk->rtj', pieces, block.astype(jnp.float32), precision=lax.Precision.HIGHEST)
            onehot = (rows_here[:, None] == row_ids[None, :]).astype(jnp.float32) * live_here[:, None]
            part = jnp.einsum('rtj,ts->rsj', contrib, onehot, precision=lax.Precision.HIGHEST).reshape(width, row_span)
            start = i_row * row_span
            current = lax.dynamic_slice_in_dim(total, start, row_span, 1)
            return lax.dynamic_update_slice_in_dim(total, current + part, start, 1), None
        total = jnp.zeros((width, NCON), jnp.float32)
        total, _ = lax.scan(visit, total, (device_ids, tile_sets, row_sets, col_sets, live_sets))
        return total

    def adjoint(vector):
        def visit(total, item):
            device, block, rows_here, cols_here, live_here = item
            i_row = (device // N_COL).astype(jnp.int32)
            j_col = (device % N_COL).astype(jnp.int32)
            source = lax.dynamic_slice_in_dim(vector, i_row * row_span, row_span, 1)
            pieces = source.reshape(width, ROWT, 128)[:, rows_here].astype(jnp.float32)
            contrib = jnp.einsum('rtj,tjk->rtk', pieces, block.astype(jnp.float32), precision=lax.Precision.HIGHEST)
            onehot = (cols_here[:, None] == col_ids[None, :]).astype(jnp.float32) * live_here[:, None]
            part = jnp.einsum('rtk,ts->rsk', contrib, onehot, precision=lax.Precision.HIGHEST).reshape(width, col_span)
            start = j_col * col_span
            current = lax.dynamic_slice_in_dim(total, start, col_span, 1)
            return lax.dynamic_update_slice_in_dim(total, current + part, start, 1), None
        total = jnp.zeros((width, NVAR), jnp.float32)
        total, _ = lax.scan(visit, total, (device_ids, tile_sets, row_sets, col_sets, live_sets))
        return total

    state_x = primal
    state_y = dual
    for step in range(ITERS):
        grad_part = adjoint(state_y.astype(jnp.bfloat16))
        x_new = jnp.clip(state_x - PRIMAL_STEP * (cost - grad_part), 0.0, upper[None, :])
        xbar = (2.0 * x_new - state_x).astype(jnp.bfloat16)
        image = forward(xbar)
        y_new = state_y + DUAL_STEP * (rhs[None, :] - image)
        y_new = jnp.where(row_kind[None, :] == 1, jnp.maximum(y_new, 0.0), y_new)
        state_x = x_new
        state_y = y_new
    return state_x, state_y
```

```python
import jax
import jax.numpy as jnp
from jax import lax
from jax.sharding import PartitionSpec as P

ITERS = 2
PRIMAL_STEP = 0.4
DUAL_STEP = 0.4
LANES = 128


def to_all(piece, axis):
    copies = jnp.broadcast_to(piece[None], (lax.axis_size(axis), *piece.shape))
    return lax.all_to_all(copies, axis, 0, 0, tiled=True)


def to_owners(parts, axis):
    return jnp.sum(lax.all_to_all(parts, axis, 0, 0, tiled=True).astype(jnp.float32), axis=0)


def as_tiles(slabs):
    devices, width, lanes = slabs.shape
    tiles = slabs.reshape(devices, width, lanes // LANES, LANES).transpose(0, 2, 1, 3)
    return tiles.reshape(-1, width, LANES)


def as_slabs(sums, devices):
    count, width, lanes = sums.shape
    slabs = sums.reshape(devices, count // devices, width, lanes).transpose(0, 2, 1, 3)
    return slabs.reshape(devices, width, -1)


def place(contrib, where, live, count):
    onehot = ((where[:, None] == jnp.arange(count, dtype=jnp.int32)[None, :]) & live[:, None]).astype(jnp.float32)
    return jnp.einsum("trj,ts->srj", contrib, onehot, precision=lax.Precision.HIGHEST)


def body(primal, dual, cost, upper, rhs, row_kind, tiles, tile_rows, tile_cols, tile_count):
    row_devices = lax.axis_size("row")
    col_devices = lax.axis_size("col")
    col_tiles = primal.shape[1] * row_devices // LANES
    row_tiles = dual.shape[1] * col_devices // LANES
    live = jnp.arange(tiles.shape[0], dtype=jnp.int32) < tile_count[0]
    x, y = primal, dual
    for _ in range(ITERS):
        y_rows = as_tiles(to_all(y.astype(jnp.bfloat16), "col"))
        contrib = jnp.einsum("trj,tjk->trk", y_rows[tile_rows], tiles, preferred_element_type=jnp.float32)
        grad = to_owners(as_slabs(place(contrib, tile_cols, live, col_tiles), row_devices), "row")
        x_new = jnp.clip(x - PRIMAL_STEP * (cost - grad), 0.0, upper[None, :])
        xbar = (2.0 * x_new - x).astype(jnp.bfloat16)
        x_cols = as_tiles(to_all(xbar, "row"))
        contrib = jnp.einsum("trk,tjk->trj", x_cols[tile_cols], tiles, preferred_element_type=jnp.float32)
        image = to_owners(as_slabs(place(contrib, tile_rows, live, row_tiles), col_devices), "col")
        y_new = y + DUAL_STEP * (rhs[None, :] - image)
        y = jnp.where(row_kind[None, :] == 1, jnp.maximum(y_new, 0.0), y_new)
        x = x_new
    return x, y


def solution(mesh):
    in_specs = (
        P(None, ("col", "row")),
        P(None, ("row", "col")),
        P(None, ("col", "row")),
        P(("col", "row")),
        P(("row", "col")),
        P(("row", "col")),
        P(("row", "col"), None, None),
        P(("row", "col")),
        P(("row", "col")),
        P(("row", "col")),
    )
    out_specs = (P(None, ("col", "row")), P(None, ("row", "col")))
    return jax.shard_map(body, mesh=mesh, in_specs=in_specs, out_specs=out_specs, check_vma=False)
```

```python
import jax
import jax.numpy as jnp
from jax import lax
from jax.sharding import PartitionSpec as P

ITERS = 2
PRIMAL_STEP = 0.4
DUAL_STEP = 0.4
LANES = 128


def to_all(piece, axis):
    copies = jnp.broadcast_to(piece[None], (lax.axis_size(axis), *piece.shape))
    return lax.all_to_all(copies, axis, 0, 0, tiled=True)


def to_owners(parts, axis):
    got = lax.all_to_all(parts.astype(jnp.bfloat16), axis, 0, 0, tiled=True)
    return jnp.sum(got.astype(jnp.float32), axis=0)


def as_tiles(slabs):
    devices, width, lanes = slabs.shape
    tiles = slabs.reshape(devices, width, lanes // LANES, LANES).transpose(0, 2, 1, 3)
    return tiles.reshape(-1, width, LANES)


def as_slabs(sums, devices):
    count, width, lanes = sums.shape
    slabs = sums.reshape(devices, count // devices, width, lanes).transpose(0, 2, 1, 3)
    return slabs.reshape(devices, width, -1)


def place(contrib, where, live, count):
    onehot = ((where[:, None] == jnp.arange(count, dtype=jnp.int32)[None, :]) & live[:, None]).astype(jnp.float32)
    return jnp.einsum("trj,ts->srj", contrib, onehot, precision=lax.Precision.HIGHEST)


def body(primal, dual, cost, upper, rhs, row_kind, tiles, tile_rows, tile_cols, tile_count):
    row_devices = lax.axis_size("row")
    col_devices = lax.axis_size("col")
    col_tiles = primal.shape[1] * row_devices // LANES
    row_tiles = dual.shape[1] * col_devices // LANES
    live = jnp.arange(tiles.shape[0], dtype=jnp.int32) < tile_count[0]
    x, y = primal, dual
    for _ in range(ITERS):
        y_rows = as_tiles(to_all(y.astype(jnp.bfloat16), "col"))
        contrib = jnp.einsum("trj,tjk->trk", y_rows[tile_rows], tiles, preferred_element_type=jnp.float32)
        grad = to_owners(as_slabs(place(contrib, tile_cols, live, col_tiles), row_devices), "row")
        x_new = jnp.clip(x - PRIMAL_STEP * (cost - grad), 0.0, upper[None, :])
        xbar = (2.0 * x_new - x).astype(jnp.bfloat16)
        x_cols = as_tiles(to_all(xbar, "row"))
        contrib = jnp.einsum("trk,tjk->trj", x_cols[tile_cols], tiles, preferred_element_type=jnp.float32)
        image = to_owners(as_slabs(place(contrib, tile_rows, live, row_tiles), col_devices), "col")
        y_new = y + DUAL_STEP * (rhs[None, :] - image)
        y = jnp.where(row_kind[None, :] == 1, jnp.maximum(y_new, 0.0), y_new)
        x = x_new
    return x, y


def solution(mesh):
    in_specs = (
        P(None, ("col", "row")),
        P(None, ("row", "col")),
        P(None, ("col", "row")),
        P(("col", "row")),
        P(("row", "col")),
        P(("row", "col")),
        P(("row", "col"), None, None),
        P(("row", "col")),
        P(("row", "col")),
        P(("row", "col")),
    )
    out_specs = (P(None, ("col", "row")), P(None, ("row", "col")))
    return jax.shard_map(body, mesh=mesh, in_specs=in_specs, out_specs=out_specs, check_vma=False)
```

```python
import functools
import math

import jax
import jax.numpy as jnp
from jax import lax
from jax.experimental import pallas as pl
from jax.experimental.pallas import tpu as pltpu
from jax.sharding import Mesh, PartitionSpec as P

ITERS = 2
PRIMAL_STEP = 0.4
DUAL_STEP = 0.4
LANES = 128
CORES = 2
TILE_MAX, UPPER_MAX, DUAL_MAX, RHS_MAX = 0.125, 1.5, 1.0, 6.0
HALF_MAX = 65504.0


def step_down(bound):
    return 2.0 ** min(0, math.floor(math.log2(0.95 * HALF_MAX / bound)))


def to_all(piece, axis):
    copies = jnp.broadcast_to(piece[None], (lax.axis_size(axis), *piece.shape))
    return lax.all_to_all(copies, axis, 0, 0, tiled=True)


def tiles_kernel(contract, from_ref, to_ref, count_ref, source_ref, tiles_ref, out_ref):
    parts = out_ref.shape[-1] // LANES
    source_parts = source_ref.shape[-1] // LANES
    out_ref[...] = jnp.zeros_like(out_ref)
    for slot in range(tiles_ref.shape[0]):
        origin, target = from_ref[slot], to_ref[slot]
        lanes = pl.ds(pl.multiple_of((origin % source_parts) * LANES, LANES), LANES)
        product = lax.dot_general(
            source_ref[origin // source_parts, :, lanes],
            tiles_ref[slot],
            (((1,), (contract,)), ((), ())),
            preferred_element_type=jnp.float32,
        )
        product = jnp.where(slot < count_ref[0], product, 0.0)
        lanes = pl.ds(pl.multiple_of((target % parts) * LANES, LANES), LANES)
        out_ref[target // parts, :, lanes] += product


def tile_products(contract, origin, target, count, source, tiles, slabs):
    smem, vmem = pl.BlockSpec(memory_space=pltpu.SMEM), pl.BlockSpec(memory_space=pltpu.VMEM)
    slots, width, lanes = tiles.shape[0], source.shape[1], source.shape[2]
    return pl.pallas_call(
        functools.partial(tiles_kernel, contract),
        out_shape=jax.ShapeDtypeStruct((slabs, width, lanes), jnp.float32),
        in_specs=[smem, smem, smem, vmem, vmem],
        out_specs=vmem,
        cost_estimate=pl.CostEstimate(
            flops=2 * slots * width * LANES * LANES, bytes_accessed=tiles.size * 2, transcendentals=0
        ),
        compiler_params=pltpu.CompilerParams(vmem_limit_bytes=16 * 2**20),
    )(origin, target, count, source, tiles)


def split(value):
    high = lax.reduce_precision(value, 5, 10)
    return high.astype(jnp.float16), (value - high).astype(jnp.float16)


def body(primal, dual, cost, upper, rhs, row_kind, tiles, tile_rows, tile_cols, tile_count):
    planes = lax.axis_size("z")
    col_devices = lax.axis_size("col")
    slots, width, piece = tiles.shape[0], primal.shape[0], primal.shape[1]
    per_piece = piece // LANES
    col_tiles = per_piece * planes * CORES
    row_tiles = per_piece * col_devices
    core = lax.axis_index("core")
    owner = tile_cols // per_piece
    tile_at = ((owner % CORES) * planes + owner // CORES) * per_piece + tile_cols % per_piece

    limits = jnp.pad(jnp.stack(split(upper)), ((0, width - 2), (0, 0)))
    state = lax.optimization_barrier(jnp.stack([*split(primal), *split(cost), limits]))

    y = dual
    y_max = DUAL_MAX
    x_half = None
    for _ in range(ITERS):
        y_rows = to_all(y.astype(jnp.bfloat16), "col")
        partial_grad = tile_products(0, tile_rows, tile_at, tile_count, y_rows, tiles, CORES * planes)

        both = lax.all_gather(partial_grad, "core", axis=0).reshape(CORES, CORES, planes, width, piece)
        mine = jnp.sum(lax.dynamic_index_in_dim(both, core, 1, keepdims=False), axis=0)
        scale = step_down(CORES * min(slots, row_tiles) * LANES * TILE_MAX * y_max)
        sends = (mine * scale).astype(jnp.float16)
        if x_half is None:
            sends = jnp.concatenate([sends, state])
        got = to_all(sends, "z")
        grad = jnp.sum(got[:, :planes].astype(jnp.float32), axis=0) * (1.0 / scale)
        if x_half is None:
            x_half = got[:, planes].astype(jnp.float32) + got[:, planes + 1].astype(jnp.float32)
            cost_half = got[:, planes + 2].astype(jnp.float32) + got[:, planes + 3].astype(jnp.float32)
            bounds = got[:, planes + 4].astype(jnp.float32)
            upper_half = bounds[:, 0:1] + bounds[:, 1:2]

        x_new = jnp.clip(x_half - PRIMAL_STEP * (cost_half - grad), 0.0, upper_half)
        xbar = (2.0 * x_new - x_half).astype(jnp.bfloat16)
        x_cols = lax.all_gather(xbar, "core", axis=0, tiled=True)
        partial_image = tile_products(1, tile_at, tile_rows, tile_count, x_cols, tiles, col_devices)
        h_max = min(slots, col_tiles) * LANES * TILE_MAX * 2 * UPPER_MAX
        scale = step_down(h_max)
        got = lax.all_to_all((partial_image * scale).astype(jnp.float16), "col", 0, 0, tiled=True)
        image = jnp.sum(got.astype(jnp.float32), axis=0) * (1.0 / scale)
        y_new = y + DUAL_STEP * (rhs[None, :] - image)
        y = jnp.where(row_kind[None, :] == 1, jnp.maximum(y_new, 0.0), y_new)
        y_max = y_max + DUAL_STEP * (RHS_MAX + col_devices * h_max)
        x_half = x_new
    return lax.dynamic_index_in_dim(x_half, lax.axis_index("z"), 0, keepdims=False), y


def solution(mesh):
    rows, cols = mesh.devices.shape
    split_mesh = Mesh(mesh.devices.reshape(rows // CORES, CORES, cols), ("z", "core", "col"))
    by_col, by_row = ("col", "z", "core"), ("z", "core", "col")
    in_specs = (
        P(None, by_col),
        P(None, by_row),
        P(None, by_col),
        P(by_col),
        P(by_row),
        P(by_row),
        P(by_row, None, None),
        P(by_row),
        P(by_row),
        P(by_row),
    )
    out_specs = (P(None, by_col), P(None, by_row))
    return jax.shard_map(body, mesh=split_mesh, in_specs=in_specs, out_specs=out_specs, check_vma=False)
```

```python
import functools
import math

import jax
import jax.numpy as jnp
from jax import lax
from jax.experimental import pallas as pl
from jax.experimental.pallas import tpu as pltpu
from jax.sharding import Mesh, PartitionSpec as P

ITERS = 2
PRIMAL_STEP = 0.4
DUAL_STEP = 0.4
LANES = 128
CORES = 2
TILE_MAX, UPPER_MAX, DUAL_MAX, RHS_MAX = 0.125, 1.5, 1.0, 6.0
HALF_MAX = 65504.0
ROW_AT, COL_AT, PLANE = range(3)


def step_down(bound):
    return 2.0 ** min(0, math.floor(math.log2(0.95 * HALF_MAX / bound)))


def to_all(piece, axis, dtype):
    copies = jnp.broadcast_to(piece[None], (lax.axis_size(axis), *piece.shape)).astype(dtype)
    return lax.all_to_all(copies, axis, 0, 0, tiled=True)


def tiles_kernel(contract, origins, targets, index_ref, source_ref, tiles_ref, *refs):
    state_ref, out_ref, own_ref, products_ref = refs if len(refs) == 4 else (None, refs[0], None, refs[1])
    parts = out_ref.shape[-1] // LANES
    source_parts = source_ref.shape[-1] // LANES
    if state_ref is not None:
        own_ref[...] = state_ref[index_ref[PLANE, 0]]
    out_ref[...] = jnp.zeros_like(out_ref)
    slots = tiles_ref.shape[0]
    for slot in range(slots):
        origin = index_ref[origins, slot]
        lanes = pl.ds(pl.multiple_of((origin % source_parts) * LANES, LANES), LANES)
        products_ref[slot] = lax.dot_general(
            source_ref[origin // source_parts, :, lanes],
            tiles_ref[slot],
            (((1,), (contract,)), ((), ())),
            preferred_element_type=jnp.float32,
        )
    for slot in range(slots):
        target = index_ref[targets, slot]
        lanes = pl.ds(pl.multiple_of((target % parts) * LANES, LANES), LANES)
        out_ref[target // parts, :, lanes] += products_ref[slot]


def tile_products(contract, origins, targets, index, source, tiles, slabs, state=None):
    smem, vmem = pl.BlockSpec(memory_space=pltpu.SMEM), pl.BlockSpec(memory_space=pltpu.VMEM)
    slots, width, lanes = tiles.shape[0], source.shape[1], source.shape[2]
    out = jax.ShapeDtypeStruct((slabs, width, lanes), jnp.float32)
    own = jax.ShapeDtypeStruct((width, lanes), jnp.float32)
    extra = () if state is None else (state,)
    return pl.pallas_call(
        functools.partial(tiles_kernel, contract, origins, targets),
        out_shape=out if state is None else (out, own),
        in_specs=[smem, vmem, vmem] + [vmem] * len(extra),
        out_specs=vmem if state is None else (vmem, vmem),
        scratch_shapes=[pltpu.VMEM((slots, width, LANES), jnp.float32)],
        cost_estimate=pl.CostEstimate(
            flops=2 * slots * width * LANES * LANES, bytes_accessed=tiles.size * 2, transcendentals=0
        ),
        compiler_params=pltpu.CompilerParams(vmem_limit_bytes=16 * 2**20),
    )(index, source, tiles, *extra)


def split(value):
    high = lax.reduce_precision(value, 5, 10)
    return high.astype(jnp.float16), (value - high).astype(jnp.float16)


def body(primal, dual, cost, upper, rhs, row_kind, tiles, tile_rows, tile_cols, tile_count):
    planes = lax.axis_size("z")
    col_devices = lax.axis_size("col")
    slots, width, piece = tiles.shape[0], primal.shape[0], primal.shape[1]
    per_piece = piece // LANES
    col_tiles = per_piece * planes * CORES
    row_tiles = per_piece * col_devices
    core = lax.axis_index("core")
    owner = tile_cols // per_piece
    tile_at = ((owner % CORES) * planes + owner // CORES) * per_piece + tile_cols % per_piece

    index = jnp.stack([tile_rows, tile_at, jnp.full_like(tile_rows, lax.axis_index("z"))])
    live = jnp.arange(slots, dtype=jnp.int32) < tile_count[0]
    tiles = jnp.where(live[:, None, None], tiles, jnp.zeros_like(tiles))

    limits = jnp.pad(jnp.stack(split(upper)), ((0, width - 2), (0, 0)))
    state = lax.optimization_barrier(jnp.stack([*split(primal), *split(cost), limits]))

    pull = jnp.broadcast_to(DUAL_STEP * rhs[None, :], dual.shape)
    floor = jnp.broadcast_to(jnp.where(row_kind == 1, 0.0, jnp.finfo(jnp.float32).min)[None, :], dual.shape)
    lifted = lax.optimization_barrier(dual) + pull
    y_sends = dual
    y_max = DUAL_MAX
    x_half = None
    for step in range(ITERS):
        y_rows = to_all(y_sends, "col", jnp.bfloat16)
        if step == 0:
            y_rows, index, tiles, state, lifted, pull, floor = lax.optimization_barrier(
                (y_rows, index, tiles, state, lifted, pull, floor)
            )
        partial_grad = tile_products(0, ROW_AT, COL_AT, index, y_rows, tiles, CORES * planes)

        both = lax.all_gather(partial_grad, "core", axis=0).reshape(CORES, CORES, planes, width, piece)
        mine = jnp.sum(lax.dynamic_index_in_dim(both, core, 1, keepdims=False), axis=0)
        scale = step_down(CORES * min(slots, row_tiles) * LANES * TILE_MAX * y_max)
        sends = (mine * scale).astype(jnp.float16)
        if step == 0:
            sends = jnp.concatenate([sends, state])
        got = to_all(sends, "z", jnp.float16)
        grad = jnp.sum(got[:, :planes].astype(jnp.float32), axis=0) * (1.0 / scale)
        if step == 0:
            x_half = got[:, planes].astype(jnp.float32) + got[:, planes + 1].astype(jnp.float32)
            cost_half = got[:, planes + 2].astype(jnp.float32) + got[:, planes + 3].astype(jnp.float32)
            bounds = got[:, planes + 4].astype(jnp.float32)
            upper_half = bounds[:, 0:1] + bounds[:, 1:2]

        x_new = jnp.clip(x_half - PRIMAL_STEP * (cost_half - grad), 0.0, upper_half)
        xbar = (2.0 * x_new - x_half).astype(jnp.bfloat16)
        x_cols = lax.all_gather(xbar, "core", axis=0, tiled=True)
        last = step == ITERS - 1
        partial_image = tile_products(1, COL_AT, ROW_AT, index, x_cols, tiles, col_devices, x_new if last else None)
        if last:
            partial_image, primal_out = partial_image
        h_max = min(slots, col_tiles) * LANES * TILE_MAX * 2 * UPPER_MAX
        scale = step_down(h_max)
        got = lax.all_to_all((partial_image * scale).astype(jnp.float16), "col", 0, 0, tiled=True)
        image = jnp.sum(got.astype(jnp.float32), axis=0)
        y = jnp.maximum(lifted - (DUAL_STEP / scale) * image, floor)
        y_max = y_max + DUAL_STEP * (RHS_MAX + col_devices * h_max)
        y_sends, lifted, x_half = y, y + pull, x_new
    return primal_out, y


def solution(mesh):
    rows, cols = mesh.devices.shape
    split_mesh = Mesh(mesh.devices.reshape(rows // CORES, CORES, cols), ("z", "core", "col"))
    by_col, by_row = ("col", "z", "core"), ("z", "core", "col")
    in_specs = (
        P(None, by_col),
        P(None, by_row),
        P(None, by_col),
        P(by_col),
        P(by_row),
        P(by_row),
        P(by_row, None, None),
        P(by_row),
        P(by_row),
        P(by_row),
    )
    out_specs = (P(None, by_col), P(None, by_row))
    return jax.shard_map(body, mesh=split_mesh, in_specs=in_specs, out_specs=out_specs, check_vma=False)
```

```python
import functools
import math

import jax
import jax.numpy as jnp
from jax import lax
from jax.experimental import pallas as pl
from jax.experimental.pallas import tpu as pltpu
from jax.sharding import Mesh, PartitionSpec as P

ITERS = 2
PRIMAL_STEP = 0.4
DUAL_STEP = 0.4
LANES = 128
CORES = 2
TILE_MAX, UPPER_MAX, DUAL_MAX, RHS_MAX = 0.125, 1.5, 1.0, 6.0
HALF_MAX = 65504.0
ROW_AT, COL_AT = range(2)


def step_down(bound):
    return 2.0 ** min(0, math.floor(math.log2(0.95 * HALF_MAX / bound)))


def to_all(piece, axis, dtype):
    copies = jnp.broadcast_to(piece[None], (lax.axis_size(axis), *piece.shape)).astype(dtype)
    return lax.all_to_all(copies, axis, 0, 0, tiled=True)


def pack(parts):
    size = sum(part.shape[0] for part in parts)
    total, at = 0.0, 0
    for part in parts:
        rest = [(0, 0)] * (part.ndim - 1)
        total = total + jnp.pad(part, [(at, size - at - part.shape[0]), *rest])
        at += part.shape[0]
    return lax.optimization_barrier(total)


def tiles_kernel(contract, origins, targets, index_ref, source_ref, tiles_ref, *refs):
    state_ref, out_ref, own_ref, products_ref = refs if len(refs) == 4 else (None, refs[0], None, refs[1])
    slots = tiles_ref.shape[0]
    width, lanes = out_ref.shape[1], out_ref.shape[2]
    if state_ref is not None:
        own_ref[...] = state_ref[lax.axis_index("z")]

    def place(row, slot):
        spot, parts = index_ref[row, slot], lanes // LANES
        return spot // parts, slice(None), pl.ds(pl.multiple_of((spot % parts) * LANES, LANES), LANES)

    def product(piece, tile):
        return lax.dot_general(piece, tile, (((1,), (contract,)), ((), ())), preferred_element_type=jnp.float32)

    out_ref[...] = jnp.zeros_like(out_ref)
    together = 2 if contract == 1 and slots % 2 == 0 else 1
    for slot in range(0, slots, together):
        pieces = [source_ref[place(origins, slot + i)] for i in range(together)]
        tiles = [tiles_ref[slot + i] for i in range(together)]
        found = product(jnp.concatenate(pieces, 0), jnp.concatenate(tiles, 0)) if together > 1 else product(pieces[0], tiles[0])
        for i in range(together):
            products_ref[slot + i] = found[i * width : (i + 1) * width, i * LANES : (i + 1) * LANES]
    for slot in range(slots):
        out_ref[place(targets, slot)] += products_ref[slot]


def tile_products(contract, origins, targets, index, source, tiles, slabs, state=None):
    smem, vmem = pl.BlockSpec(memory_space=pltpu.SMEM), pl.BlockSpec(memory_space=pltpu.VMEM)
    slots, width, lanes = tiles.shape[0], source.shape[1], source.shape[2]
    out = jax.ShapeDtypeStruct((slabs, width, lanes), jnp.float32)
    own = jax.ShapeDtypeStruct((width, lanes), jnp.float32)
    extra = () if state is None else (state,)
    return pl.pallas_call(
        functools.partial(tiles_kernel, contract, origins, targets),
        out_shape=out if state is None else (out, own),
        in_specs=[smem, vmem, vmem] + [vmem] * len(extra),
        out_specs=vmem if state is None else (vmem, vmem),
        scratch_shapes=[pltpu.VMEM((slots, width, LANES), jnp.float32)],
        cost_estimate=pl.CostEstimate(
            flops=2 * slots * width * LANES * LANES, bytes_accessed=tiles.size * 2, transcendentals=0
        ),
        compiler_params=pltpu.CompilerParams(vmem_limit_bytes=16 * 2**20),
    )(index, source, tiles, *extra)


def split(value):
    high = lax.reduce_precision(value, 5, 10)
    return high.astype(jnp.float16), (value - high).astype(jnp.float16)


def body(primal, dual, cost, upper, rhs, row_kind, tiles, tile_rows, tile_cols, tile_count):
    planes = lax.axis_size("z")
    col_devices = lax.axis_size("col")
    slots, width, piece = tiles.shape[0], primal.shape[0], primal.shape[1]
    per_piece = piece // LANES
    col_tiles = per_piece * planes * CORES
    row_tiles = per_piece * col_devices
    core = lax.axis_index("core")
    owner = tile_cols // per_piece
    tile_at = ((owner % CORES) * planes + owner // CORES) * per_piece + tile_cols % per_piece
    index = jnp.stack([tile_rows, tile_at])
    live = jnp.arange(slots, dtype=jnp.int32) < tile_count[0]
    tiles = jnp.where(live[:, None, None], tiles, jnp.zeros_like(tiles))

    floor = jnp.where(row_kind == 1, 0.0, jnp.finfo(jnp.float32).min)
    x_own, cost_own, y = jnp.split(pack([primal, cost, lax.optimization_barrier(dual)]), 3)
    vectors = jnp.split(pack([upper, rhs, floor]), 3)
    upper_own, rhs_own, floor = (jnp.broadcast_to(vector[None], primal.shape) for vector in vectors)
    first_row = lax.broadcasted_iota(jnp.int32, primal.shape, 0) == 0
    state = jnp.stack([*split(x_own), *split(cost_own), jnp.where(first_row, *split(upper_own))])
    pull = DUAL_STEP * rhs_own
    lifted = y + pull
    y_sends = dual
    y_max = DUAL_MAX
    x_half = None
    for step in range(ITERS):
        y_rows = to_all(y_sends, "col", jnp.bfloat16)
        if step == 0:
            y_rows, index, tiles, state, lifted, pull, floor = lax.optimization_barrier(
                (y_rows, index, tiles, state, lifted, pull, floor)
            )
        partial_grad = tile_products(0, ROW_AT, COL_AT, index, y_rows, tiles, CORES * planes)

        both = lax.all_gather(partial_grad, "core", axis=0).reshape(CORES, CORES, planes, width, piece)
        mine = jnp.sum(lax.dynamic_index_in_dim(both, core, 1, keepdims=False), axis=0)
        scale = step_down(CORES * min(slots, row_tiles) * LANES * TILE_MAX * y_max)
        sends = (mine * scale).astype(jnp.float16)
        if step == 0:
            sends = jnp.concatenate([sends, state])
        got = to_all(sends, "z", jnp.float16)
        grad = jnp.sum(got[:, :planes].astype(jnp.float32), axis=0) * (1.0 / scale)
        if step == 0:
            x_half = got[:, planes].astype(jnp.float32) + got[:, planes + 1].astype(jnp.float32)
            cost_half = got[:, planes + 2].astype(jnp.float32) + got[:, planes + 3].astype(jnp.float32)
            bounds = got[:, planes + 4].astype(jnp.float32)
            upper_half = bounds[:, 0:1] + bounds[:, 1:2]

        x_new = jnp.clip(x_half - PRIMAL_STEP * (cost_half - grad), 0.0, upper_half)
        xbar = (2.0 * x_new - x_half).astype(jnp.bfloat16)
        x_cols = lax.all_gather(xbar, "core", axis=0, tiled=True)
        last = step == ITERS - 1
        partial_image = tile_products(1, COL_AT, ROW_AT, index, x_cols, tiles, col_devices, x_new if last else None)
        if last:
            partial_image, primal_out = partial_image
        h_max = min(slots, col_tiles) * LANES * TILE_MAX * 2 * UPPER_MAX
        scale = step_down(h_max)
        got = lax.all_to_all((partial_image * scale).astype(jnp.float16), "col", 0, 0, tiled=True)
        image = jnp.sum(got.astype(jnp.float32), axis=0)
        y = jnp.maximum(lifted - (DUAL_STEP / scale) * image, floor)
        y_max = y_max + DUAL_STEP * (RHS_MAX + col_devices * h_max)
        y_sends, lifted, x_half = y, y + pull, x_new
    return primal_out, y


def solution(mesh):
    rows, cols = mesh.devices.shape
    split_mesh = Mesh(mesh.devices.reshape(rows // CORES, CORES, cols), ("z", "core", "col"))
    by_col, by_row = ("col", "z", "core"), ("z", "core", "col")
    in_specs = (
        P(None, by_col),
        P(None, by_row),
        P(None, by_col),
        P(by_col),
        P(by_row),
        P(by_row),
        P(by_row, None, None),
        P(by_row),
        P(by_row),
        P(by_row),
    )
    out_specs = (P(None, by_col), P(None, by_row))
    return jax.shard_map(body, mesh=split_mesh, in_specs=in_specs, out_specs=out_specs, check_vma=False)
```

```python
import functools
import math

import jax
import jax.numpy as jnp
from jax import lax
from jax.experimental import pallas as pl
from jax.experimental.pallas import tpu as pltpu
from jax.sharding import Mesh, PartitionSpec as P

ITERS = 2
PRIMAL_STEP = 0.4
DUAL_STEP = 0.4
LANES = 128
CORES = 2
TILE_MAX, UPPER_MAX, DUAL_MAX, RHS_MAX = 0.125, 1.5, 1.0, 6.0
HALF_MAX = 65504.0
ROW_AT, COL_AT = range(2)


def step_down(bound):
    return 2.0 ** min(0, math.floor(math.log2(0.95 * HALF_MAX / bound)))


def to_all(piece, axis, dtype, fresh=False):
    zeros = lax.optimization_barrier(jnp.zeros((lax.axis_size(axis), 1, 1), piece.dtype)) if fresh else 0.0
    copies = jnp.broadcast_to(piece[None] + zeros, (lax.axis_size(axis), *piece.shape)).astype(dtype)
    return lax.all_to_all(copies, axis, 0, 0, tiled=True)


def pack(parts):
    size = sum(part.shape[0] for part in parts)
    total, at = 0, 0
    for part in parts:
        rest = [(0, 0)] * (part.ndim - 1)
        total = total + jnp.pad(part, [(at, size - at - part.shape[0]), *rest])
        at += part.shape[0]
    return lax.optimization_barrier(total)


def tiles_kernel(contract, origins, targets, index_ref, source_ref, tiles_ref, out_ref, products_ref):
    slots = tiles_ref.shape[0]
    width, lanes = out_ref.shape[1], out_ref.shape[2]

    def place(row, slot):
        spot, parts = index_ref[row, slot], lanes // LANES
        return spot // parts, slice(None), pl.ds(pl.multiple_of((spot % parts) * LANES, LANES), LANES)

    def product(piece, tile):
        return lax.dot_general(piece, tile, (((1,), (contract,)), ((), ())), preferred_element_type=jnp.float32)

    out_ref[...] = jnp.zeros_like(out_ref)
    together = 2 if contract == 1 and slots % 2 == 0 else 1
    for slot in range(0, slots, together):
        pieces = [source_ref[place(origins, slot + i)] for i in range(together)]
        tiles = [tiles_ref[slot + i] for i in range(together)]
        found = product(jnp.concatenate(pieces, 0), jnp.concatenate(tiles, 0)) if together > 1 else product(pieces[0], tiles[0])
        for i in range(together):
            products_ref[slot + i] = found[i * width : (i + 1) * width, i * LANES : (i + 1) * LANES]
    for slot in range(slots):
        out_ref[place(targets, slot)] += products_ref[slot]


def tile_products(contract, origins, targets, index, source, tiles, slabs):
    smem, vmem = pl.BlockSpec(memory_space=pltpu.SMEM), pl.BlockSpec(memory_space=pltpu.VMEM)
    slots, width, lanes = tiles.shape[0], source.shape[1], source.shape[2]
    return pl.pallas_call(
        functools.partial(tiles_kernel, contract, origins, targets),
        out_shape=jax.ShapeDtypeStruct((slabs, width, lanes), jnp.float32),
        in_specs=[smem, vmem, vmem],
        out_specs=vmem,
        scratch_shapes=[pltpu.VMEM((slots, width, LANES), jnp.float32)],
        cost_estimate=pl.CostEstimate(
            flops=2 * slots * width * LANES * LANES, bytes_accessed=tiles.size * 2, transcendentals=0
        ),
        compiler_params=pltpu.CompilerParams(vmem_limit_bytes=16 * 2**20),
    )(index, source, tiles)


def results_kernel(steps, lifted_ref, pull_ref, floor_ref, x_ref, *refs):
    *image_refs, primal_ref, dual_ref = refs
    primal_ref[...] = x_ref[lax.axis_index("z")]
    lifted = lifted_ref[...]
    for step, image_ref in zip(steps, image_refs):
        y = jnp.maximum(lifted - step * image_ref[...], floor_ref[...])
        lifted = y + pull_ref[...]
    dual_ref[...] = y


def results(steps, lifted, pull, floor, x_half, images):
    vmem = pl.BlockSpec(memory_space=pltpu.VMEM)
    return pl.pallas_call(
        functools.partial(results_kernel, steps),
        out_shape=(jax.ShapeDtypeStruct(lifted.shape, jnp.float32),) * 2,
        in_specs=[vmem] * (4 + len(images)),
        out_specs=(vmem, vmem),
        compiler_params=pltpu.CompilerParams(vmem_limit_bytes=16 * 2**20),
    )(lifted, pull, floor, x_half, *images)


def split(value):
    high = lax.reduce_precision(value, 5, 10)
    return high.astype(jnp.float16), (value - high).astype(jnp.float16)


def body(primal, dual, cost, upper, rhs, row_kind, tiles, tile_rows, tile_cols, tile_count):
    planes = lax.axis_size("z")
    col_devices = lax.axis_size("col")
    slots, width, piece = tiles.shape[0], primal.shape[0], primal.shape[1]
    per_piece = piece // LANES
    col_tiles = per_piece * planes * CORES
    row_tiles = per_piece * col_devices
    core = lax.axis_index("core")
    live = jnp.arange(slots, dtype=jnp.int32) < tile_count[0]
    tiles = jnp.where(live[:, None, None], tiles, jnp.zeros_like(tiles))

    x_own, cost_own, y = jnp.split(pack([primal, cost, lax.optimization_barrier(dual)]), 3)
    upper_own, rhs_own = jnp.split(pack([upper, rhs]), 2)
    kind, rows, cols = jnp.split(pack([row_kind, tile_rows, tile_cols]), [piece, piece + slots])
    floor = jnp.where(kind == 1, 0.0, jnp.finfo(jnp.float32).min)
    upper_own, rhs_own, floor = (jnp.broadcast_to(vector[None], primal.shape) for vector in (upper_own, rhs_own, floor))
    owner = cols // per_piece
    tile_at = ((owner % CORES) * planes + owner // CORES) * per_piece + cols % per_piece
    index = jnp.stack([rows, tile_at])

    first_row = lax.broadcasted_iota(jnp.int32, primal.shape, 0) == 0
    state = jnp.stack([*split(x_own), *split(cost_own), jnp.where(first_row, *split(upper_own))])
    pull = DUAL_STEP * rhs_own
    lifted = y + pull
    y_sends = dual
    y_max = DUAL_MAX
    x_half = None
    for step in range(ITERS):
        y_rows = to_all(y_sends, "col", jnp.bfloat16, fresh=step == 0)
        if step == 0:
            y_rows, index, tiles, state, lifted, pull, floor = lax.optimization_barrier(
                (y_rows, index, tiles, state, lifted, pull, floor)
            )
            raised, images, steps = lifted, [], []
        partial_grad = tile_products(0, ROW_AT, COL_AT, index, y_rows, tiles, CORES * planes)

        both = lax.all_gather(partial_grad, "core", axis=0).reshape(CORES, CORES, planes, width, piece)
        mine = jnp.sum(lax.dynamic_index_in_dim(both, core, 1, keepdims=False), axis=0)
        scale = step_down(CORES * min(slots, row_tiles) * LANES * TILE_MAX * y_max)
        sends = (mine * scale).astype(jnp.float16)
        if step == 0:
            sends = jnp.concatenate([sends, state])
        got = to_all(sends, "z", jnp.float16)
        grad = jnp.sum(got[:, :planes].astype(jnp.float32), axis=0) * (1.0 / scale)
        if step == 0:
            x_half = got[:, planes].astype(jnp.float32) + got[:, planes + 1].astype(jnp.float32)
            cost_half = got[:, planes + 2].astype(jnp.float32) + got[:, planes + 3].astype(jnp.float32)
            bounds = got[:, planes + 4].astype(jnp.float32)
            upper_half = bounds[:, 0:1] + bounds[:, 1:2]

        x_new = jnp.clip(x_half - PRIMAL_STEP * (cost_half - grad), 0.0, upper_half)
        xbar = (2.0 * x_new - x_half).astype(jnp.bfloat16)
        x_cols = lax.all_gather(xbar, "core", axis=0, tiled=True)
        partial_image = tile_products(1, COL_AT, ROW_AT, index, x_cols, tiles, col_devices)
        h_max = min(slots, col_tiles) * LANES * TILE_MAX * 2 * UPPER_MAX
        scale = step_down(h_max)
        got = lax.all_to_all((partial_image * scale).astype(jnp.float16), "col", 0, 0, tiled=True)
        image = jnp.sum(got.astype(jnp.float32), axis=0)
        images.append(image)
        steps.append(DUAL_STEP / scale)
        y = jnp.maximum(raised - steps[-1] * image, floor)
        y_max = y_max + DUAL_STEP * (RHS_MAX + col_devices * h_max)
        y_sends, raised, x_half = y, y + pull, x_new
    return results(tuple(steps), lifted, pull, floor, x_half, images)


def solution(mesh):
    rows, cols = mesh.devices.shape
    split_mesh = Mesh(mesh.devices.reshape(rows // CORES, CORES, cols), ("z", "core", "col"))
    by_col, by_row = ("col", "z", "core"), ("z", "core", "col")
    in_specs = (
        P(None, by_col),
        P(None, by_row),
        P(None, by_col),
        P(by_col),
        P(by_row),
        P(by_row),
        P(by_row, None, None),
        P(by_row),
        P(by_row),
        P(by_row),
    )
    out_specs = (P(None, by_col), P(None, by_row))
    return jax.shard_map(body, mesh=split_mesh, in_specs=in_specs, out_specs=out_specs, check_vma=False)
```

```python
import functools
import math

import jax
import jax.numpy as jnp
from jax import lax
from jax.experimental import pallas as pl
from jax.experimental.pallas import tpu as pltpu
from jax.sharding import Mesh, PartitionSpec as P

ITERS = 2
PRIMAL_STEP = 0.4
DUAL_STEP = 0.4
LANES = 128
CORES = 2
TILE_MAX, UPPER_MAX, DUAL_MAX, RHS_MAX = 0.125, 1.5, 1.0, 6.0
HALF_MAX = 65504.0
ROW_AT, COL_AT = range(2)


def step_down(bound):
    return 2.0 ** min(0, math.floor(math.log2(0.95 * HALF_MAX / bound)))


def to_all(piece, axis, dtype, fresh=False):
    zeros = lax.optimization_barrier(jnp.zeros((lax.axis_size(axis), 1, 1), piece.dtype)) if fresh else 0.0
    copies = jnp.broadcast_to(piece[None] + zeros, (lax.axis_size(axis), *piece.shape)).astype(dtype)
    return lax.all_to_all(copies, axis, 0, 0, tiled=True)


def pack(parts):
    size = sum(part.shape[0] for part in parts)
    total, at = 0, 0
    for part in parts:
        rest = [(0, 0)] * (part.ndim - 1)
        total = total + jnp.pad(part, [(at, size - at - part.shape[0]), *rest])
        at += part.shape[0]
    return lax.optimization_barrier(total)


def tiles_kernel(contract, origins, targets, index_ref, source_ref, tiles_ref, out_ref, products_ref):
    slots = tiles_ref.shape[0]
    width, lanes = out_ref.shape[1], out_ref.shape[2]

    def place(row, slot):
        spot, parts = index_ref[row, slot], lanes // LANES
        return spot // parts, slice(None), pl.ds(pl.multiple_of((spot % parts) * LANES, LANES), LANES)

    def product(piece, tile):
        return lax.dot_general(piece, tile, (((1,), (contract,)), ((), ())), preferred_element_type=jnp.float32)

    out_ref[...] = jnp.zeros_like(out_ref)
    together = 2 if contract == 1 and slots % 2 == 0 else 1
    for slot in range(0, slots, together):
        pieces = [source_ref[place(origins, slot + i)] for i in range(together)]
        tiles = [tiles_ref[slot + i] for i in range(together)]
        found = product(jnp.concatenate(pieces, 0), jnp.concatenate(tiles, 0)) if together > 1 else product(pieces[0], tiles[0])
        for i in range(together):
            products_ref[slot + i] = found[i * width : (i + 1) * width, i * LANES : (i + 1) * LANES]
    for slot in range(slots):
        out_ref[place(targets, slot)] += products_ref[slot]


def tile_products(contract, origins, targets, index, source, tiles, slabs):
    smem, vmem = pl.BlockSpec(memory_space=pltpu.SMEM), pl.BlockSpec(memory_space=pltpu.VMEM)
    slots, width, lanes = tiles.shape[0], source.shape[1], source.shape[2]
    return pl.pallas_call(
        functools.partial(tiles_kernel, contract, origins, targets),
        out_shape=jax.ShapeDtypeStruct((slabs, width, lanes), jnp.float32),
        in_specs=[smem, vmem, vmem],
        out_specs=vmem,
        scratch_shapes=[pltpu.VMEM((slots, width, LANES), jnp.float32)],
        cost_estimate=pl.CostEstimate(
            flops=2 * slots * width * LANES * LANES, bytes_accessed=tiles.size * 2, transcendentals=0
        ),
        compiler_params=pltpu.CompilerParams(vmem_limit_bytes=16 * 2**20),
    )(index, source, tiles)


def results_kernel(steps, lifted_ref, pull_ref, floor_ref, x_ref, *refs):
    *image_refs, primal_ref, dual_ref = refs
    primal_ref[...] = x_ref[lax.axis_index("z")]
    lifted = lifted_ref[...]
    for step, image_ref in zip(steps, image_refs):
        y = jnp.maximum(lifted - step * image_ref[...], floor_ref[...])
        lifted = y + pull_ref[...]
    dual_ref[...] = y


def results(steps, lifted, pull, floor, x_half, images):
    vmem = pl.BlockSpec(memory_space=pltpu.VMEM)
    return pl.pallas_call(
        functools.partial(results_kernel, steps),
        out_shape=(jax.ShapeDtypeStruct(lifted.shape, jnp.float32),) * 2,
        in_specs=[vmem] * (4 + len(images)),
        out_specs=(vmem, vmem),
        compiler_params=pltpu.CompilerParams(vmem_limit_bytes=16 * 2**20),
    )(lifted, pull, floor, x_half, *images)


def split(value):
    high = lax.reduce_precision(value, 5, 10)
    return high.astype(jnp.float16), (value - high).astype(jnp.float16)


def body(primal, dual, cost, upper, rhs, row_kind, tiles, tile_rows, tile_cols, tile_count):
    planes = lax.axis_size("z")
    col_devices = lax.axis_size("col")
    slots, width, piece = tiles.shape[0], primal.shape[0], primal.shape[1]
    per_piece = piece // LANES
    col_tiles = per_piece * planes * CORES
    row_tiles = per_piece * col_devices
    core = lax.axis_index("core")
    live = jnp.arange(slots, dtype=jnp.int32) < tile_count[0]
    tiles = jnp.where(live[:, None, None], tiles, jnp.zeros_like(tiles))

    fields = pack([primal, cost, lax.optimization_barrier(dual), upper[None], rhs[None]])
    x_own, cost_own, y, upper_own, rhs_own = jnp.split(fields, [width, 2 * width, 3 * width, 3 * width + 1])
    kind, rows, cols = jnp.split(pack([row_kind, tile_rows, tile_cols]), [piece, piece + slots])
    floor = jnp.where(kind == 1, 0.0, jnp.finfo(jnp.float32).min)
    upper_own, rhs_own, floor = (jnp.broadcast_to(row, primal.shape) for row in (upper_own, rhs_own, floor[None]))
    owner = cols // per_piece
    tile_at = ((owner % CORES) * planes + owner // CORES) * per_piece + cols % per_piece
    index = jnp.stack([rows, tile_at])

    first_row = lax.broadcasted_iota(jnp.int32, primal.shape, 0) == 0
    state = jnp.stack([*split(x_own), *split(cost_own), jnp.where(first_row, *split(upper_own))])
    pull = DUAL_STEP * rhs_own
    lifted = y + pull
    y_sends = dual
    y_max = DUAL_MAX
    x_half = None
    for step in range(ITERS):
        y_rows = to_all(y_sends, "col", jnp.bfloat16, fresh=step == 0)
        if step == 0:
            y_rows, index, tiles, state, lifted, pull, floor = lax.optimization_barrier(
                (y_rows, index, tiles, state, lifted, pull, floor)
            )
            raised, images, steps = lifted, [], []
        partial_grad = tile_products(0, ROW_AT, COL_AT, index, y_rows, tiles, CORES * planes)

        both = lax.all_gather(partial_grad, "core", axis=0).reshape(CORES, CORES, planes, width, piece)
        mine = jnp.sum(lax.dynamic_index_in_dim(both, core, 1, keepdims=False), axis=0)
        scale = step_down(CORES * min(slots, row_tiles) * LANES * TILE_MAX * y_max)
        sends = (mine * scale).astype(jnp.float16)
        if step == 0:
            sends = jnp.concatenate([sends, state])
        got = to_all(sends, "z", jnp.float16)
        grad = jnp.sum(got[:, :planes].astype(jnp.float32), axis=0) * (1.0 / scale)
        if step == 0:
            x_half = got[:, planes].astype(jnp.float32) + got[:, planes + 1].astype(jnp.float32)
            cost_half = got[:, planes + 2].astype(jnp.float32) + got[:, planes + 3].astype(jnp.float32)
            bounds = got[:, planes + 4].astype(jnp.float32)
            upper_half = bounds[:, 0:1] + bounds[:, 1:2]

        x_new = jnp.clip(x_half - PRIMAL_STEP * (cost_half - grad), 0.0, upper_half)
        xbar = (2.0 * x_new - x_half).astype(jnp.bfloat16)
        x_cols = lax.all_gather(xbar, "core", axis=0, tiled=True)
        partial_image = tile_products(1, COL_AT, ROW_AT, index, x_cols, tiles, col_devices)
        h_max = min(slots, col_tiles) * LANES * TILE_MAX * 2 * UPPER_MAX
        scale = step_down(h_max)
        got = lax.all_to_all((partial_image * scale).astype(jnp.float16), "col", 0, 0, tiled=True)
        image = jnp.sum(got.astype(jnp.float32), axis=0)
        images.append(image)
        steps.append(DUAL_STEP / scale)
        y = jnp.maximum(raised - steps[-1] * image, floor)
        y_max = y_max + DUAL_STEP * (RHS_MAX + col_devices * h_max)
        y_sends, raised, x_half = y, y + pull, x_new
    return results(tuple(steps), lifted, pull, floor, x_half, images)


def solution(mesh):
    rows, cols = mesh.devices.shape
    split_mesh = Mesh(mesh.devices.reshape(rows // CORES, CORES, cols), ("z", "core", "col"))
    by_col, by_row = ("col", "z", "core"), ("z", "core", "col")
    in_specs = (
        P(None, by_col),
        P(None, by_row),
        P(None, by_col),
        P(by_col),
        P(by_row),
        P(by_row),
        P(by_row, None, None),
        P(by_row),
        P(by_row),
        P(by_row),
    )
    out_specs = (P(None, by_col), P(None, by_row))
    return jax.shard_map(body, mesh=split_mesh, in_specs=in_specs, out_specs=out_specs, check_vma=False)
```

```python
import functools
import math

import jax
import jax.numpy as jnp
from jax import lax
from jax.experimental import pallas as pl
from jax.experimental.pallas import tpu as pltpu
from jax.sharding import Mesh, PartitionSpec as P

ITERS = 2
PRIMAL_STEP = 0.4
DUAL_STEP = 0.4
LANES = 128
CORES = 2
TILE_MAX, UPPER_MAX, DUAL_MAX, RHS_MAX = 0.125, 1.5, 1.0, 6.0
HALF_MAX = 65504.0
ROW_AT, COL_AT = range(2)


def step_down(bound):
    return 2.0 ** min(0, math.floor(math.log2(0.95 * HALF_MAX / bound)))


def to_all(piece, axis, dtype, fresh=False):
    zeros = lax.optimization_barrier(jnp.zeros((lax.axis_size(axis), 1, 1), piece.dtype)) if fresh else 0.0
    copies = jnp.broadcast_to(piece[None] + zeros, (lax.axis_size(axis), *piece.shape)).astype(dtype)
    return lax.all_to_all(copies, axis, 0, 0, tiled=True)


def pack(parts):
    rows, lanes = sum(part.shape[0] for part in parts), max(part.shape[1] for part in parts)
    total, at = 0.0, 0
    for part in parts:
        padded = jnp.pad(part, ((at, rows - at - part.shape[0]), (0, lanes - part.shape[1])))
        total = total + padded.astype(jnp.float32)
        at += part.shape[0]
    return lax.optimization_barrier(total)


def tiles_kernel(contract, origins, targets, index_ref, source_ref, tiles_ref, out_ref, products_ref):
    slots = tiles_ref.shape[0]
    width, lanes = out_ref.shape[1], out_ref.shape[2]

    def place(row, slot):
        spot, parts = index_ref[row, slot], lanes // LANES
        return spot // parts, slice(None), pl.ds(pl.multiple_of((spot % parts) * LANES, LANES), LANES)

    def product(piece, tile):
        return lax.dot_general(piece, tile, (((1,), (contract,)), ((), ())), preferred_element_type=jnp.float32)

    out_ref[...] = jnp.zeros_like(out_ref)
    together = 2 if contract == 1 and slots % 2 == 0 else 1
    for slot in range(0, slots, together):
        pieces = [source_ref[place(origins, slot + i)] for i in range(together)]
        tiles = [tiles_ref[slot + i] for i in range(together)]
        found = product(jnp.concatenate(pieces, 0), jnp.concatenate(tiles, 0)) if together > 1 else product(pieces[0], tiles[0])
        for i in range(together):
            products_ref[slot + i] = found[i * width : (i + 1) * width, i * LANES : (i + 1) * LANES]
    for slot in range(slots):
        out_ref[place(targets, slot)] += products_ref[slot]


def tile_products(contract, origins, targets, index, source, tiles, slabs):
    smem, vmem = pl.BlockSpec(memory_space=pltpu.SMEM), pl.BlockSpec(memory_space=pltpu.VMEM)
    slots, width, lanes = tiles.shape[0], source.shape[1], source.shape[2]
    return pl.pallas_call(
        functools.partial(tiles_kernel, contract, origins, targets),
        out_shape=jax.ShapeDtypeStruct((slabs, width, lanes), jnp.float32),
        in_specs=[smem, vmem, vmem],
        out_specs=vmem,
        scratch_shapes=[pltpu.VMEM((slots, width, LANES), jnp.float32)],
        cost_estimate=pl.CostEstimate(
            flops=2 * slots * width * LANES * LANES, bytes_accessed=tiles.size * 2, transcendentals=0
        ),
        compiler_params=pltpu.CompilerParams(vmem_limit_bytes=16 * 2**20),
    )(index, source, tiles)


def results_kernel(steps, lifted_ref, pull_ref, floor_ref, x_ref, *refs):
    *image_refs, primal_ref, dual_ref = refs
    primal_ref[...] = x_ref[lax.axis_index("z")]
    lifted = lifted_ref[...]
    for step, image_ref in zip(steps, image_refs):
        y = jnp.maximum(lifted - step * image_ref[...], floor_ref[...])
        lifted = y + pull_ref[...]
    dual_ref[...] = y


def results(steps, lifted, pull, floor, x_half, images):
    vmem = pl.BlockSpec(memory_space=pltpu.VMEM)
    return pl.pallas_call(
        functools.partial(results_kernel, steps),
        out_shape=(jax.ShapeDtypeStruct(lifted.shape, jnp.float32),) * 2,
        in_specs=[vmem] * (4 + len(images)),
        out_specs=(vmem, vmem),
        compiler_params=pltpu.CompilerParams(vmem_limit_bytes=16 * 2**20),
    )(lifted, pull, floor, x_half, *images)


def split(value):
    high = lax.reduce_precision(value, 5, 10)
    return high.astype(jnp.float16), (value - high).astype(jnp.float16)


def body(primal, dual, cost, upper, rhs, row_kind, tiles, tile_rows, tile_cols, tile_count):
    planes = lax.axis_size("z")
    col_devices = lax.axis_size("col")
    slots, width, piece = tiles.shape[0], primal.shape[0], primal.shape[1]
    per_piece = piece // LANES
    col_tiles = per_piece * planes * CORES
    row_tiles = per_piece * col_devices
    core = lax.axis_index("core")
    live = jnp.arange(slots, dtype=jnp.int32) < tile_count[0]
    tiles = jnp.where(live[:, None, None], tiles, jnp.zeros_like(tiles))

    rows_of = [upper, rhs, row_kind, tile_rows, tile_cols]
    fields = pack([primal, cost, lax.optimization_barrier(dual), *(vector[None] for vector in rows_of)])
    ends = [width, 2 * width, *(3 * width + i for i in range(len(rows_of)))]
    x_own, cost_own, y, upper_own, rhs_own, kind, rows, cols = jnp.split(fields, ends)
    rows, cols = (row[0, :slots].astype(jnp.int32) for row in (rows, cols))
    floor = jnp.where(kind == 1.0, 0.0, jnp.finfo(jnp.float32).min)
    upper_own, rhs_own, floor = (jnp.broadcast_to(row, primal.shape) for row in (upper_own, rhs_own, floor))
    owner = cols // per_piece
    tile_at = ((owner % CORES) * planes + owner // CORES) * per_piece + cols % per_piece
    index = jnp.stack([rows, tile_at])

    first_row = lax.broadcasted_iota(jnp.int32, primal.shape, 0) == 0
    state = jnp.stack([*split(x_own), *split(cost_own), jnp.where(first_row, *split(upper_own))])
    pull = DUAL_STEP * rhs_own
    lifted = y + pull
    y_sends = dual
    y_max = DUAL_MAX
    x_half = None
    for step in range(ITERS):
        y_rows = to_all(y_sends, "col", jnp.bfloat16, fresh=step == 0)
        if step == 0:
            y_rows, index, tiles, state, lifted, pull, floor = lax.optimization_barrier(
                (y_rows, index, tiles, state, lifted, pull, floor)
            )
            raised, images, steps = lifted, [], []
        partial_grad = tile_products(0, ROW_AT, COL_AT, index, y_rows, tiles, CORES * planes)

        both = lax.all_gather(partial_grad, "core", axis=0).reshape(CORES, CORES, planes, width, piece)
        mine = jnp.sum(lax.dynamic_index_in_dim(both, core, 1, keepdims=False), axis=0)
        scale = step_down(CORES * min(slots, row_tiles) * LANES * TILE_MAX * y_max)
        sends = (mine * scale).astype(jnp.float16)
        if step == 0:
            sends = jnp.concatenate([sends, state])
        got = to_all(sends, "z", jnp.float16)
        grad = jnp.sum(got[:, :planes].astype(jnp.float32), axis=0) * (1.0 / scale)
        if step == 0:
            x_half = got[:, planes].astype(jnp.float32) + got[:, planes + 1].astype(jnp.float32)
            cost_half = got[:, planes + 2].astype(jnp.float32) + got[:, planes + 3].astype(jnp.float32)
            bounds = got[:, planes + 4].astype(jnp.float32)
            upper_half = bounds[:, 0:1] + bounds[:, 1:2]

        x_new = jnp.clip(x_half - PRIMAL_STEP * (cost_half - grad), 0.0, upper_half)
        xbar = (2.0 * x_new - x_half).astype(jnp.bfloat16)
        x_cols = lax.all_gather(xbar, "core", axis=0, tiled=True)
        partial_image = tile_products(1, COL_AT, ROW_AT, index, x_cols, tiles, col_devices)
        h_max = min(slots, col_tiles) * LANES * TILE_MAX * 2 * UPPER_MAX
        scale = step_down(h_max)
        got = lax.all_to_all((partial_image * scale).astype(jnp.float16), "col", 0, 0, tiled=True)
        image = jnp.sum(got.astype(jnp.float32), axis=0)
        images.append(image)
        steps.append(DUAL_STEP / scale)
        y = jnp.maximum(raised - steps[-1] * image, floor)
        y_max = y_max + DUAL_STEP * (RHS_MAX + col_devices * h_max)
        y_sends, raised, x_half = y, y + pull, x_new
    return results(tuple(steps), lifted, pull, floor, x_half, images)


def solution(mesh):
    rows, cols = mesh.devices.shape
    split_mesh = Mesh(mesh.devices.reshape(rows // CORES, CORES, cols), ("z", "core", "col"))
    by_col, by_row = ("col", "z", "core"), ("z", "core", "col")
    in_specs = (
        P(None, by_col),
        P(None, by_row),
        P(None, by_col),
        P(by_col),
        P(by_row),
        P(by_row),
        P(by_row, None, None),
        P(by_row),
        P(by_row),
        P(by_row),
    )
    out_specs = (P(None, by_col), P(None, by_row))
    return jax.shard_map(body, mesh=split_mesh, in_specs=in_specs, out_specs=out_specs, check_vma=False)
```

```python
import functools
import math

import jax
import jax.numpy as jnp
from jax import lax
from jax.experimental import pallas as pl
from jax.experimental.pallas import tpu as pltpu
from jax.sharding import Mesh, PartitionSpec as P

ITERS = 2
PRIMAL_STEP = 0.4
DUAL_STEP = 0.4
LANES = 128
CORES = 2
TILE_MAX, UPPER_MAX, DUAL_MAX, RHS_MAX = 0.125, 1.5, 1.0, 6.0
HALF_MAX = 65504.0
ROW_AT, COL_AT = range(2)


def step_down(bound):
    return 2.0 ** min(0, math.floor(math.log2(0.95 * HALF_MAX / bound)))


def to_all(piece, axis, dtype):
    copies = jnp.broadcast_to(piece[None], (lax.axis_size(axis), *piece.shape)).astype(dtype)
    return lax.all_to_all(copies, axis, 0, 0, tiled=True)


def pack(parts):
    rows, lanes = sum(part.shape[0] for part in parts), max(part.shape[1] for part in parts)
    total, at = 0.0, 0
    for part in parts:
        padded = jnp.pad(part, ((at, rows - at - part.shape[0]), (0, lanes - part.shape[1])))
        total = total + padded.astype(jnp.float32)
        at += part.shape[0]
    return lax.optimization_barrier(total)


def tiles_kernel(contract, origins, targets, index_ref, source_ref, tiles_ref, out_ref, products_ref):
    slots = tiles_ref.shape[0]
    width, lanes = out_ref.shape[1], out_ref.shape[2]

    def place(row, slot):
        spot, parts = index_ref[row, slot], lanes // LANES
        return spot // parts, slice(None), pl.ds(pl.multiple_of((spot % parts) * LANES, LANES), LANES)

    def product(piece, tile):
        return lax.dot_general(piece, tile, (((1,), (contract,)), ((), ())), preferred_element_type=jnp.float32)

    out_ref[...] = jnp.zeros_like(out_ref)
    together = 2 if slots % 2 == 0 else 1
    for slot in range(0, slots, together):
        pieces = [source_ref[place(origins, slot + i)] for i in range(together)]
        tiles = [tiles_ref[slot + i] for i in range(together)]
        found = product(jnp.concatenate(pieces, 0), jnp.concatenate(tiles, 1 - contract)) if together > 1 else product(pieces[0], tiles[0])
        for i in range(together):
            products_ref[slot + i] = found[i * width : (i + 1) * width, i * LANES : (i + 1) * LANES]
    for slot in range(slots):
        out_ref[place(targets, slot)] += products_ref[slot]


def tile_products(contract, origins, targets, index, source, tiles, slabs):
    smem, vmem = pl.BlockSpec(memory_space=pltpu.SMEM), pl.BlockSpec(memory_space=pltpu.VMEM)
    slots, width, lanes = tiles.shape[0], source.shape[1], source.shape[2]
    return pl.pallas_call(
        functools.partial(tiles_kernel, contract, origins, targets),
        out_shape=jax.ShapeDtypeStruct((slabs, width, lanes), jnp.float32),
        in_specs=[smem, vmem, vmem],
        out_specs=vmem,
        scratch_shapes=[pltpu.VMEM((slots, width, LANES), jnp.float32)],
        cost_estimate=pl.CostEstimate(
            flops=2 * slots * width * LANES * LANES, bytes_accessed=tiles.size * 2, transcendentals=0
        ),
        compiler_params=pltpu.CompilerParams(vmem_limit_bytes=16 * 2**20),
    )(index, source, tiles)


def results_kernel(steps, lifted_ref, pull_ref, floor_ref, x_ref, *refs):
    *image_refs, primal_ref, dual_ref = refs
    primal_ref[...] = x_ref[lax.axis_index("z")]
    lifted = lifted_ref[...]
    for step, image_ref in zip(steps, image_refs):
        y = jnp.maximum(lifted - step * image_ref[...], floor_ref[...])
        lifted = y + pull_ref[...]
    dual_ref[...] = y


def results(steps, lifted, pull, floor, x_half, images):
    vmem = pl.BlockSpec(memory_space=pltpu.VMEM)
    return pl.pallas_call(
        functools.partial(results_kernel, steps),
        out_shape=(jax.ShapeDtypeStruct(lifted.shape, jnp.float32),) * 2,
        in_specs=[vmem] * (4 + len(images)),
        out_specs=(vmem, vmem),
        compiler_params=pltpu.CompilerParams(vmem_limit_bytes=16 * 2**20),
    )(lifted, pull, floor, x_half, *images)


def split(value):
    high = lax.reduce_precision(value, 5, 10)
    return high.astype(jnp.float16), (value - high).astype(jnp.float16)


def body(primal, dual, cost, upper, rhs, row_kind, tiles, tile_rows, tile_cols, tile_count):
    planes = lax.axis_size("z")
    col_devices = lax.axis_size("col")
    slots, width, piece = tiles.shape[0], primal.shape[0], primal.shape[1]
    per_piece = piece // LANES
    col_tiles = per_piece * planes * CORES
    row_tiles = per_piece * col_devices
    core = lax.axis_index("core")
    live = jnp.arange(slots, dtype=jnp.int32) < tile_count[0]
    tiles = jnp.where(live[:, None, None], tiles, jnp.zeros_like(tiles))

    rows_of = [upper, rhs, row_kind, tile_rows, tile_cols]
    fields = pack([primal, cost, lax.optimization_barrier(dual), *(vector[None] for vector in rows_of)])
    ends = [width, 2 * width, *(3 * width + i for i in range(len(rows_of)))]
    x_own, cost_own, y, upper_own, rhs_own, kind, rows, cols = jnp.split(fields, ends)
    rows, cols = (row[0, :slots].astype(jnp.int32) for row in (rows, cols))
    floor = jnp.where(kind == 1.0, 0.0, jnp.finfo(jnp.float32).min)
    upper_own, rhs_own, floor = (jnp.broadcast_to(row, primal.shape) for row in (upper_own, rhs_own, floor))
    owner = cols // per_piece
    tile_at = ((owner % CORES) * planes + owner // CORES) * per_piece + cols % per_piece
    index = jnp.stack([rows, tile_at])

    first_row = lax.broadcasted_iota(jnp.int32, primal.shape, 0) == 0
    state = jnp.stack([*split(x_own), *split(cost_own), jnp.where(first_row, *split(upper_own))])
    pull = DUAL_STEP * rhs_own
    lifted = y + pull
    y_sends = dual
    y_max = DUAL_MAX
    x_half = None
    for step in range(ITERS):
        y_rows = to_all(y_sends, "col", jnp.bfloat16)
        if step == 0:
            y_rows, index, tiles, state, lifted, pull, floor = lax.optimization_barrier(
                (y_rows, index, tiles, state, lifted, pull, floor)
            )
            raised, images, steps = lifted, [], []
        partial_grad = tile_products(0, ROW_AT, COL_AT, index, y_rows, tiles, CORES * planes)

        halves = partial_grad.reshape(CORES, planes, width, piece)
        passed = lax.all_gather(lax.dynamic_index_in_dim(halves, 1 - core, 0, keepdims=False), "core", axis=0)
        mine = sum(lax.dynamic_index_in_dim(part, at, 0, keepdims=False) for part, at in ((halves, core), (passed, 1 - core)))
        scale = step_down(CORES * min(slots, row_tiles) * LANES * TILE_MAX * y_max)
        sends = (mine * scale).astype(jnp.float16)
        if step == 0:
            sends = jnp.concatenate([sends, state])
        got = to_all(sends, "z", jnp.float16)
        grad = jnp.sum(got[:, :planes].astype(jnp.float32), axis=0) * (1.0 / scale)
        if step == 0:
            x_half = got[:, planes].astype(jnp.float32) + got[:, planes + 1].astype(jnp.float32)
            cost_half = got[:, planes + 2].astype(jnp.float32) + got[:, planes + 3].astype(jnp.float32)
            bounds = got[:, planes + 4].astype(jnp.float32)
            upper_half = bounds[:, 0:1] + bounds[:, 1:2]

        x_new = jnp.clip(x_half - PRIMAL_STEP * (cost_half - grad), 0.0, upper_half)
        xbar = (2.0 * x_new - x_half).astype(jnp.bfloat16)
        x_cols = lax.all_gather(xbar, "core", axis=0, tiled=True)
        partial_image = tile_products(1, COL_AT, ROW_AT, index, x_cols, tiles, col_devices)
        h_max = min(slots, col_tiles) * LANES * TILE_MAX * 2 * UPPER_MAX
        scale = step_down(h_max)
        got = lax.all_to_all((partial_image * scale).astype(jnp.float16), "col", 0, 0, tiled=True)
        image = jnp.sum(got.astype(jnp.float32), axis=0)
        images.append(image)
        steps.append(DUAL_STEP / scale)
        y = jnp.maximum(raised - steps[-1] * image, floor)
        y_max = y_max + DUAL_STEP * (RHS_MAX + col_devices * h_max)
        y_sends, raised, x_half = y, y + pull, x_new
    return results(tuple(steps), lifted, pull, floor, x_half, images)


def solution(mesh):
    rows, cols = mesh.devices.shape
    split_mesh = Mesh(mesh.devices.reshape(rows // CORES, CORES, cols), ("z", "core", "col"))
    by_col, by_row = ("col", "z", "core"), ("z", "core", "col")
    in_specs = (
        P(None, by_col),
        P(None, by_row),
        P(None, by_col),
        P(by_col),
        P(by_row),
        P(by_row),
        P(by_row, None, None),
        P(by_row),
        P(by_row),
        P(by_row),
    )
    out_specs = (P(None, by_col), P(None, by_row))
    return jax.shard_map(body, mesh=split_mesh, in_specs=in_specs, out_specs=out_specs, check_vma=False)
```

```python
import functools
import math

import jax
import jax.numpy as jnp
from jax import lax
from jax.experimental import pallas as pl
from jax.experimental.pallas import tpu as pltpu
from jax.sharding import Mesh, PartitionSpec as P

ITERS = 2
PRIMAL_STEP = 0.4
DUAL_STEP = 0.4
LANES = 128
CORES = 2
TILE_MAX, UPPER_MAX, DUAL_MAX, RHS_MAX = 0.125, 1.5, 1.0, 6.0
HALF_MAX = 65504.0
ROW_AT, COL_AT = range(2)


def step_down(bound):
    return 2.0 ** min(0, math.floor(math.log2(0.95 * HALF_MAX / bound)))


def to_all(piece, axis, dtype):
    copies = jnp.broadcast_to(piece[None], (lax.axis_size(axis), *piece.shape)).astype(dtype)
    return lax.all_to_all(copies, axis, 0, 0, tiled=True)


def pack(parts):
    rows, lanes = sum(part.shape[0] for part in parts), max(part.shape[1] for part in parts)
    total, at = 0.0, 0
    for part in parts:
        padded = jnp.pad(part, ((at, rows - at - part.shape[0]), (0, lanes - part.shape[1])))
        total = total + padded.astype(jnp.float32)
        at += part.shape[0]
    return lax.optimization_barrier(total)


def tiles_kernel(contract, origins, targets, index_ref, source_ref, tiles_ref, out_ref, products_ref):
    slots = tiles_ref.shape[0]
    width, lanes = out_ref.shape[1], out_ref.shape[2]

    def place(row, slot):
        spot, parts = index_ref[row, slot], lanes // LANES
        return spot // parts, slice(None), pl.ds(pl.multiple_of((spot % parts) * LANES, LANES), LANES)

    def product(piece, tile):
        return lax.dot_general(piece, tile, (((1,), (contract,)), ((), ())), preferred_element_type=jnp.float32)

    out_ref[...] = jnp.zeros_like(out_ref)
    together = 2 if slots % 2 == 0 else 1
    for slot in range(0, slots, together):
        pieces = [source_ref[place(origins, slot + i)] for i in range(together)]
        tiles = [tiles_ref[slot + i] for i in range(together)]
        found = product(jnp.concatenate(pieces, 0), jnp.concatenate(tiles, 1 - contract)) if together > 1 else product(pieces[0], tiles[0])
        for i in range(together):
            products_ref[slot + i] = found[i * width : (i + 1) * width, i * LANES : (i + 1) * LANES]
    for slot in range(slots):
        out_ref[place(targets, slot)] += products_ref[slot]


def tile_products(contract, origins, targets, index, source, tiles, slabs):
    smem, vmem = pl.BlockSpec(memory_space=pltpu.SMEM), pl.BlockSpec(memory_space=pltpu.VMEM)
    slots, width, lanes = tiles.shape[0], source.shape[1], source.shape[2]
    return pl.pallas_call(
        functools.partial(tiles_kernel, contract, origins, targets),
        out_shape=jax.ShapeDtypeStruct((slabs, width, lanes), jnp.float32),
        in_specs=[smem, vmem, vmem],
        out_specs=vmem,
        scratch_shapes=[pltpu.VMEM((slots, width, LANES), jnp.float32)],
        cost_estimate=pl.CostEstimate(
            flops=2 * slots * width * LANES * LANES, bytes_accessed=tiles.size * 2, transcendentals=0
        ),
        compiler_params=pltpu.CompilerParams(vmem_limit_bytes=16 * 2**20),
    )(index, source, tiles)


def results_kernel(steps, lifted_ref, pull_ref, floor_ref, x_ref, *refs):
    *image_refs, primal_ref, dual_ref = refs
    primal_ref[...] = x_ref[lax.axis_index("z")]
    lifted = lifted_ref[...]
    for step, image_ref in zip(steps, image_refs):
        y = jnp.maximum(lifted - step * image_ref[...], floor_ref[...])
        lifted = y + pull_ref[...]
    dual_ref[...] = y


def results(steps, lifted, pull, floor, x_half, images):
    vmem = pl.BlockSpec(memory_space=pltpu.VMEM)
    return pl.pallas_call(
        functools.partial(results_kernel, steps),
        out_shape=(jax.ShapeDtypeStruct(lifted.shape, jnp.float32),) * 2,
        in_specs=[vmem] * (4 + len(images)),
        out_specs=(vmem, vmem),
        compiler_params=pltpu.CompilerParams(vmem_limit_bytes=16 * 2**20),
    )(lifted, pull, floor, x_half, *images)


def split(value):
    high = lax.reduce_precision(value, 5, 10)
    return high.astype(jnp.float16), (value - high).astype(jnp.float16)


def body(primal, dual, cost, upper, rhs, row_kind, tiles, tile_rows, tile_cols, tile_count):
    planes = lax.axis_size("z")
    col_devices = lax.axis_size("col")
    slots, width, piece = tiles.shape[0], primal.shape[0], primal.shape[1]
    per_piece = piece // LANES
    col_tiles = per_piece * planes * CORES
    row_tiles = per_piece * col_devices
    core = lax.axis_index("core")
    live = jnp.arange(slots, dtype=jnp.int32) < tile_count[0]
    tiles = jnp.where(live[:, None, None], tiles, jnp.zeros_like(tiles))

    rows_of = [upper, rhs, row_kind, tile_rows, tile_cols]
    fields = pack([primal, cost, lax.optimization_barrier(dual), *(vector[None] for vector in rows_of)])
    ends = [width, 2 * width, *(3 * width + i for i in range(len(rows_of)))]
    x_own, cost_own, y, upper_own, rhs_own, kind, rows, cols = jnp.split(fields, ends)
    rows, cols = (row[0, :slots].astype(jnp.int32) for row in (rows, cols))
    floor = jnp.where(kind == 1.0, 0.0, jnp.finfo(jnp.float32).min)
    upper_own, rhs_own, floor = (jnp.broadcast_to(row, primal.shape) for row in (upper_own, rhs_own, floor))
    owner = cols // per_piece
    tile_at = ((owner % CORES) * planes + owner // CORES) * per_piece + cols % per_piece
    index = jnp.stack([rows, tile_at])

    first_row = lax.broadcasted_iota(jnp.int32, primal.shape, 0) == 0
    state = jnp.stack([*split(x_own), *split(cost_own), jnp.where(first_row, *split(upper_own))])
    pull = DUAL_STEP * rhs_own
    lifted = y + pull
    y_sends = dual
    y_max = DUAL_MAX
    x_half = None
    for step in range(ITERS):
        y_rows = to_all(y_sends, "col", jnp.bfloat16)
        if step == 0:
            y_rows, index, tiles, state, lifted, pull, floor = lax.optimization_barrier(
                (y_rows, index, tiles, state, lifted, pull, floor)
            )
            raised, images, steps = lifted, [], []
        partial_grad = tile_products(0, ROW_AT, COL_AT, index, y_rows, tiles, CORES * planes)

        both = lax.all_gather(partial_grad, "core", axis=0).reshape(CORES, CORES, planes, width, piece)
        mine = jnp.sum(lax.dynamic_index_in_dim(both, core, 1, keepdims=False), axis=0)
        scale = step_down(CORES * min(slots, row_tiles) * LANES * TILE_MAX * y_max)
        sends = (mine * scale).astype(jnp.float16)
        if step == 0:
            sends = jnp.concatenate([sends, state])
        got = to_all(sends, "z", jnp.float16)
        grad = jnp.sum(got[:, :planes].astype(jnp.float32), axis=0) * (1.0 / scale)
        if step == 0:
            x_half = got[:, planes].astype(jnp.float32) + got[:, planes + 1].astype(jnp.float32)
            cost_half = got[:, planes + 2].astype(jnp.float32) + got[:, planes + 3].astype(jnp.float32)
            bounds = got[:, planes + 4].astype(jnp.float32)
            upper_half = bounds[:, 0:1] + bounds[:, 1:2]

        x_new = jnp.clip(x_half - PRIMAL_STEP * (cost_half - grad), 0.0, upper_half)
        xbar = (2.0 * x_new - x_half).astype(jnp.bfloat16)
        x_cols = lax.all_gather(xbar, "core", axis=0, tiled=True)
        partial_image = tile_products(1, COL_AT, ROW_AT, index, x_cols, tiles, col_devices)
        h_max = min(slots, col_tiles) * LANES * TILE_MAX * 2 * UPPER_MAX
        scale = step_down(h_max)
        got = lax.all_to_all((partial_image * scale).astype(jnp.float16), "col", 0, 0, tiled=True)
        image = jnp.sum(got.astype(jnp.float32), axis=0)
        images.append(image)
        steps.append(DUAL_STEP / scale)
        y = jnp.maximum(raised - steps[-1] * image, floor)
        y_max = y_max + DUAL_STEP * (RHS_MAX + col_devices * h_max)
        y_sends, raised, x_half = y, y + pull, x_new
    return results(tuple(steps), lifted, pull, floor, x_half, images)


def solution(mesh):
    rows, cols = mesh.devices.shape
    split_mesh = Mesh(mesh.devices.reshape(rows // CORES, CORES, cols), ("z", "core", "col"))
    by_col, by_row = ("col", "z", "core"), ("z", "core", "col")
    in_specs = (
        P(None, by_col),
        P(None, by_row),
        P(None, by_col),
        P(by_col),
        P(by_row),
        P(by_row),
        P(by_row, None, None),
        P(by_row),
        P(by_row),
        P(by_row),
    )
    out_specs = (P(None, by_col), P(None, by_row))
    return jax.shard_map(body, mesh=split_mesh, in_specs=in_specs, out_specs=out_specs, check_vma=False)
```
